32 devices in a mesh: dp: 4 (over x, core), frame: 2 (over y), space: 4 (over z).
Axes of the slice: x: 2, y: 2, z: 4, core: 2. Of those that a mesh axis runs over, the one named last changes fastest.
Arguments:
- clip_tokens: bfloat16 [4, 16, 1024, 1024], P('dp', 'frame', 'space'), may hold values from -6 to 6
- lookback: int32 [4], P('dp'), may hold values from 2 to 16
- valid_frames: int32 [4], P('dp'), may hold values from 1 to 16
- spatial_gain: float32 [1024], replicated, may hold values from 0.1 to 1.9
- spatial_qkv: bfloat16 [1024, 3072], P('frame'), may hold values from -1 to 1
- spatial_out: bfloat16 [1024, 1024], P('frame'), may hold values from -0.375 to 0.375
- temporal_gain: float32 [1024], replicated, may hold values from 0.1 to 1.9
- temporal_qkv: bfloat16 [1024, 3072], P('frame'), may hold values from -1 to 1
- temporal_out: bfloat16 [1024, 1024], P('frame'), may hold values from -0.375 to 0.375
- cotangent: bfloat16 [4, 16, 1024, 1024], P('dp', 'frame', 'space'), may hold values from -0.3125 to 0.3125
Outputs:
- block_out: float32 [4, 16, 1024, 1024], P('dp', 'frame', 'space')
- grad_temporal_out: float32 [1024, 1024], P('frame')
The draws below stay inside these ranges and needn't reach their ends.
All inputs are finite; a program needn't handle non-finite values.
Results may differ from the reference program's by a relative error of at most 0.039.
The reference program's roundings to bfloat16 on the way count: a program that leaves them out, or rounds other values in their place, can miss the bound.
Values may be sent and summed in bfloat16 or wider, within the bound.
A program may use at most 448 MiB of HBM per device.

```python
import jax
import jax.numpy as jnp
from jax import lax

D = 1024
H = 16
HD = 64
F = 16
P_SIZE = 1024
CLIPS = 4


def projection_draw(key):
    base = jnp.clip(jax.random.normal(key, (D, 3 * D), jnp.float32), -4.0, 4.0) * (D // 4) ** (-0.5)
    return base


def draw_spatial_qkv(key, part):
    return projection_draw(jax.random.fold_in(key, 1)).astype(jnp.bfloat16)


def draw_temporal_qkv(key, part):
    return projection_draw(jax.random.fold_in(key, 2)).astype(jnp.bfloat16)


def set_ends(drawn, stream_key, least, high):
    longest = drawn.shape.index(max(drawn.shape))
    spots = []
    for shift in (0, 1):
        where = [jax.random.randint(jax.random.fold_in(stream_key, axis), (), 0, length) for axis, length in enumerate(drawn.shape)]
        where[longest] = (where[longest] + shift) % drawn.shape[longest]
        spots.append(tuple(where))
    return drawn.at[spots[0]].set(least).at[spots[1]].set(high)


def with_spikes(values, rng, source, target, shards_of, factor):
    def block_of(axis_at):
        return (jnp.arange(values.shape[axis_at]) // (values.shape[axis_at] // shards_of)).reshape((-1,) + (1,) * (values.ndim - 1 - axis_at))

    one_side = jax.random.permutation(rng, shards_of)[block_of(target)]
    other_side = (block_of(target) + shards_of // 2) % shards_of
    return jnp.where((block_of(source) == one_side) | (block_of(source) == other_side), factor * values, values)


def shard_levels(key, shape, split, smallest, largest):
    level, own = 1.0, jax.random.fold_in(key, 6)
    for dim, blocks in split:
        heights = jnp.exp(jax.random.uniform(jax.random.fold_in(own, dim), (blocks,), jnp.float32, smallest / len(split), largest / len(split)))
        level = level * jnp.repeat(heights, shape[dim] // blocks).reshape([-1 if axis == dim else 1 for axis in range(len(shape))])
    return level


def bell_draw(own_key, extent, spread, most, shards=(), held_as=jnp.bfloat16):
    factor_of = shard_levels(own_key, extent, shards, -0.22, 0.18) if shards else 1.0
    result = jax.random.normal(own_key, extent, jnp.float32) * spread * factor_of
    return jnp.minimum(jnp.maximum(result, -most), most).astype(held_as)


def heavy_noise(rng, dims, width, most, shards, heavy, dtype=jnp.bfloat16):
    result = width * jax.random.normal(rng, dims, jnp.float32)
    if shards:
        result = result * shard_levels(rng, dims, shards, -0.22, 0.18)
    return jnp.clip(with_spikes(result, jax.random.fold_in(rng, 3), *heavy), -most, most).astype(dtype)


def setup_inputs(seed: int = 0) -> dict:
    splits = jax.random.split(jax.random.key(seed), 11)
    clip_tokens = bell_draw(splits[0], (CLIPS, F, P_SIZE, D), 1.0, 6.0, ((0, 4), (1, 2), (2, 4)))
    lookback = set_ends(jax.random.randint(splits[1], (CLIPS,), 2, F + 1), jax.random.fold_in(splits[1], 1), 2, F).astype(jnp.int32)
    valid_frames = set_ends(jax.random.randint(splits[2], (CLIPS,), 1, F + 1), jax.random.fold_in(splits[2], 1), 1, F).astype(jnp.int32)
    spatial_gain = jnp.clip(1.0 + 0.18 * jax.random.normal(splits[3], (D,), jnp.float32), 0.1, 1.9)
    spatial_qkv = draw_spatial_qkv(jax.random.fold_in(splits[10], 71), 0)
    spatial_out = bell_draw(splits[5], (D, D), (D // 4) ** -0.5, 0.375, ((0, 2),))
    temporal_gain = jnp.clip(1.0 + 0.18 * jax.random.normal(splits[6], (D,), jnp.float32), 0.1, 1.9)
    temporal_qkv = draw_temporal_qkv(jax.random.fold_in(splits[10], 71), 0)
    temporal_out = bell_draw(splits[8], (D, D), (D // 4) ** -0.5, 0.375, ((0, 2),))
    cotangent = heavy_noise(splits[9], (CLIPS, F, P_SIZE, D), ((CLIPS * F * P_SIZE) ** -0.5 * 4), 0.3125, ((0, 4), (1, 2), (2, 4)), (1, 3, 2, 2.0))
    return dict(clip_tokens=clip_tokens, lookback=lookback, valid_frames=valid_frames, spatial_gain=spatial_gain, spatial_qkv=spatial_qkv, spatial_out=spatial_out, temporal_gain=temporal_gain, temporal_qkv=temporal_qkv, temporal_out=temporal_out, cotangent=cotangent)


norm_eps = 1e-06
score_scale = 0.125

def rms_norm(row_block, gain):
    values = row_block.astype(jnp.float32)
    mean_square = lax.optimization_barrier(jnp.mean(values * values, axis=-1, keepdims=True))
    return (values * lax.rsqrt(mean_square + norm_eps) * gain).astype(jnp.bfloat16)

def rounded_back(weights):
    return lax.optimization_barrier(weights.astype(jnp.bfloat16)).astype(jnp.float32)

def spatial_frame(frame_rows, spatial_gain, spatial_qkv, spatial_out):
    normed = rms_norm(frame_rows, spatial_gain)
    projected = jnp.dot(normed, spatial_qkv, preferred_element_type=jnp.float32).astype(jnp.bfloat16)
    queries = projected[:, :D].reshape(P_SIZE, H, HD).astype(jnp.float32)
    key_rows = projected[:, D:2 * D].reshape(P_SIZE, H, HD).astype(jnp.float32)
    value_rows = projected[:, 2 * D:].reshape(P_SIZE, H, HD).astype(jnp.float32)
    scores = jnp.einsum('qhd,khd->hqk', queries, key_rows) * score_scale
    row_best = lax.optimization_barrier(jnp.max(scores, axis=-1, keepdims=True))
    attn_weights = jnp.exp(scores - row_best)
    weight_sum = lax.optimization_barrier(jnp.sum(attn_weights, axis=-1, keepdims=True))
    mixed_rows = jnp.einsum('hqk,khd->qhd', rounded_back(attn_weights), value_rows)
    mixed_rows = mixed_rows / jnp.transpose(weight_sum, (1, 0, 2))
    attended = mixed_rows.astype(jnp.bfloat16).reshape(P_SIZE, D)
    return frame_rows.astype(jnp.float32) + jnp.dot(attended, spatial_out, preferred_element_type=jnp.float32)

def one_clip(clip_rows, reach, live, cotangent_rows, spatial_gain, spatial_qkv, spatial_out, temporal_gain, temporal_qkv, temporal_out):
    after_spatial = lax.map(lambda frame_rows: spatial_frame(frame_rows, spatial_gain, spatial_qkv, spatial_out), clip_rows)
    flat_rows = after_spatial.reshape(F * P_SIZE, D)
    normed = rms_norm(flat_rows, temporal_gain)
    projected = jnp.dot(normed, temporal_qkv, preferred_element_type=jnp.float32).astype(jnp.bfloat16)
    queries = projected[:, :D].reshape(F, P_SIZE, H, HD).astype(jnp.float32)
    key_rows = projected[:, D:2 * D].reshape(F, P_SIZE, H, HD).astype(jnp.float32)
    value_rows = projected[:, 2 * D:].reshape(F, P_SIZE, H, HD).astype(jnp.float32)
    query_pos = lax.broadcasted_iota(jnp.int32, (F, F), 0)
    key_pos = lax.broadcasted_iota(jnp.int32, (F, F), 1)
    visible = (key_pos <= query_pos) & (query_pos - key_pos < reach) & ((key_pos < live) | (key_pos == query_pos))
    scores = jnp.einsum('tphd,sphd->phts', queries, key_rows) * score_scale
    row_best = lax.optimization_barrier(jnp.max(jnp.where(visible, scores, -1e+30), axis=-1, keepdims=True))
    temporal_weights = jnp.where(visible, jnp.exp(scores - row_best), 0.0)
    temporal_sum = lax.optimization_barrier(jnp.sum(temporal_weights, axis=-1))
    mixed_rows = jnp.einsum('phts,sphd->tphd', rounded_back(temporal_weights), value_rows)
    mixed_rows = mixed_rows / jnp.transpose(temporal_sum, (2, 0, 1))[..., None]
    attended = mixed_rows.astype(jnp.bfloat16).reshape(F * P_SIZE, D)
    summed = flat_rows + jnp.dot(attended, temporal_out, preferred_element_type=jnp.float32)
    block_rows = summed.reshape(F, P_SIZE, D)
    grad_rows = lax.dot_general(cotangent_rows.reshape(F * P_SIZE, D), attended, (((0,), (0,)), ((), ())), preferred_element_type=jnp.float32)
    return (block_rows, grad_rows)

def reference(clip_tokens, lookback, valid_frames, spatial_gain, spatial_qkv, spatial_out, temporal_gain, temporal_qkv, temporal_out, cotangent):

    def step_clip(inputs):
        clip_rows, reach, live, cotangent_rows = inputs
        return one_clip(clip_rows, reach, live, cotangent_rows, spatial_gain, spatial_qkv, spatial_out, temporal_gain, temporal_qkv, temporal_out)
    block_out, grads = lax.map(step_clip, (clip_tokens, lookback, valid_frames, cotangent))
    return (block_out, lax.optimization_barrier(jnp.sum(grads, axis=0)))
```

```python
import functools
import math

import jax
import jax.numpy as jnp
from jax import lax
from jax.experimental import pallas as pl
from jax.experimental.pallas import tpu as pltpu
from jax.sharding import PartitionSpec as P

HD = 64
PAIR = 2 * HD

norm_eps = 1e-06
score_scale = 0.125
exp2_scale = score_scale * math.log2(math.e)


def rms_norm(row_block, gain):
    values = row_block.astype(jnp.float32)
    mean_square = jnp.mean(values * values, axis=-1, keepdims=True)
    return (values * lax.rsqrt(mean_square + norm_eps) * gain).astype(jnp.bfloat16)


def fold_rows(activations, weight_rows):
    return jnp.dot(activations, weight_rows, preferred_element_type=jnp.float32)


def frame_visible(lookback, valid_frames, query_pos, key_pos):
    return (
        (key_pos <= query_pos)
        & (query_pos - key_pos < lookback)
        & ((key_pos < valid_frames) | (key_pos == query_pos))
    )


def pair_attention(query, key, value, bias=None):
    low_q = lax.broadcasted_iota(jnp.int32, query.shape, 1) < HD
    low_v = lax.broadcasted_iota(jnp.int32, value.shape, 1) < HD
    none = jnp.zeros_like(query)
    ones = jnp.ones_like(value)
    mixed = []
    for query_one, value_one in (
        (jnp.where(low_q, query, none), jnp.where(low_v, value, ones)),
        (jnp.where(low_q, none, query), jnp.where(low_v, ones, value)),
    ):
        scores = lax.dot_general(
            query_one, key, (((1,), (1,)), ((), ())), preferred_element_type=jnp.float32
        )
        if bias is not None:
            scores = scores + bias
        row_best = jnp.max(scores, axis=-1, keepdims=True)
        weights = jnp.exp2((scores - row_best) * exp2_scale).astype(jnp.bfloat16)
        mixed.append(jnp.dot(weights, value_one, preferred_element_type=jnp.float32))
    first, second = mixed
    top = jnp.where(low_q, first, second)
    bottom = pltpu.roll(jnp.where(low_q, second, first), HD, 1)
    return (top / bottom).astype(jnp.bfloat16)


def spatial_kernel(query_ref, key_ref, value_ref, out_ref, *, step):
    key, value = key_ref[...], value_ref[...]
    for start in range(0, query_ref.shape[0], step):
        out_ref[start : start + step, :] = pair_attention(
            query_ref[start : start + step, :], key, value
        )


def spatial_attention(projected, patches, width):
    rows = projected.shape[0]
    pairs = width // PAIR

    def block(shift):
        return pl.BlockSpec((patches, PAIR), lambda g, j: (g, j + shift * pairs))

    return pl.pallas_call(
        functools.partial(spatial_kernel, step=min(256, patches)),
        grid=(rows // patches, pairs),
        in_specs=[block(0), block(1), block(2)],
        out_specs=block(0),
        out_shape=jax.ShapeDtypeStruct((rows, width), jnp.bfloat16),
        compiler_params=pltpu.CompilerParams(vmem_limit_bytes=48 * 2**20),
        cost_estimate=pl.CostEstimate(
            flops=4 * rows * patches * width,
            bytes_accessed=8 * rows * width,
            transcendentals=rows * patches * width // HD,
        ),
    )(projected, projected, projected)


def temporal_kernel(bias_ref, rows_ref, out_ref, *, width):
    bias = bias_ref[...]
    frames, group, _ = out_ref.shape
    for start in range(0, width, PAIR):
        parts = [
            rows_ref[:, :, shift + start : shift + start + PAIR].reshape(frames * group, PAIR)
            for shift in (0, width, 2 * width)
        ]
        out_ref[:, :, start : start + PAIR] = pair_attention(*parts, bias).reshape(
            frames, group, PAIR
        )


def temporal_attention(projected, lookback, valid_frames, width):
    frames, patches, _ = projected.shape
    group = 16
    spots = frames * group
    row = lax.broadcasted_iota(jnp.int32, (spots, spots), 0)
    column = lax.broadcasted_iota(jnp.int32, (spots, spots), 1)
    seen = frame_visible(lookback, valid_frames, row // group, column // group)
    bias = jnp.where(seen & (row % group == column % group), 0.0, -1e30).astype(jnp.float32)
    return pl.pallas_call(
        functools.partial(temporal_kernel, width=width),
        grid=(patches // group,),
        in_specs=[
            pl.BlockSpec((spots, spots), lambda i: (0, 0)),
            pl.BlockSpec((frames, group, 3 * width), lambda i: (0, i, 0)),
        ],
        out_specs=pl.BlockSpec((frames, group, width), lambda i: (0, i, 0)),
        out_shape=jax.ShapeDtypeStruct((frames, patches, width), jnp.bfloat16),
        compiler_params=pltpu.CompilerParams(vmem_limit_bytes=48 * 2**20),
        cost_estimate=pl.CostEstimate(
            flops=4 * spots * frames * patches * width,
            bytes_accessed=8 * frames * patches * width,
            transcendentals=spots * frames * patches * width // HD,
        ),
    )(bias, projected)


def gather_rows(weight):
    return lax.all_gather(weight, "frame", axis=0, tiled=True)


def spatial_by_frames(tokens, gain, qkv):
    frames_here, patches_here, width = tokens.shape
    whole = lax.all_to_all(tokens, "space", split_axis=0, concat_axis=1, tiled=True)
    frames, patches, _ = whole.shape
    normed = rms_norm(whole.reshape(frames * patches, width), gain)
    projected = fold_rows(normed, qkv).astype(jnp.bfloat16)
    attended = spatial_attention(projected, patches, width).reshape(frames, patches, width)
    return lax.all_to_all(attended, "space", split_axis=1, concat_axis=0, tiled=True)


def spatial_by_heads(tokens, gain, qkv):
    frames_here, patches_here, width = tokens.shape
    parts = lax.axis_size("space")
    normed = rms_norm(tokens.reshape(-1, width), gain)
    projected = fold_rows(normed, qkv).astype(jnp.bfloat16)
    split = projected.reshape(frames_here, patches_here, 3, parts, width // parts)
    whole = lax.all_to_all(split, "space", split_axis=3, concat_axis=1, tiled=True)
    patches = whole.shape[1]
    attended = spatial_attention(
        whole.reshape(frames_here * patches, -1), patches, width // parts
    ).reshape(frames_here, patches, width // parts)
    return lax.all_to_all(attended, "space", split_axis=1, concat_axis=2, tiled=True)


def on_device(
    clip_tokens,
    lookback,
    valid_frames,
    spatial_gain,
    spatial_qkv,
    spatial_out,
    temporal_gain,
    temporal_qkv,
    temporal_out,
    cotangent,
):
    clip_count, frames_here, patches_here, width = clip_tokens.shape
    total_rows = frames_here * patches_here
    by_frames = frames_here % lax.axis_size("space") == 0
    spatial = spatial_by_frames if by_frames else spatial_by_heads
    tokens = clip_tokens[0]
    spatial_attn = spatial(tokens, spatial_gain, gather_rows(spatial_qkv))
    spatial_proj = fold_rows(spatial_attn.reshape(total_rows, width), gather_rows(spatial_out))
    after_spatial = tokens.reshape(total_rows, width).astype(jnp.float32) + spatial_proj
    normed_next = rms_norm(after_spatial, temporal_gain)
    patch_tokens = lax.all_to_all(
        normed_next.reshape(frames_here, patches_here, width),
        "frame",
        split_axis=1,
        concat_axis=0,
        tiled=True,
    )
    frames, patches, _ = patch_tokens.shape
    projected = fold_rows(
        patch_tokens.reshape(frames * patches, width), gather_rows(temporal_qkv)
    ).astype(jnp.bfloat16)
    result_rows = temporal_attention(
        projected.reshape(frames, patches, 3 * width), lookback[0], valid_frames[0], width
    )
    temporal_attn = lax.all_to_all(
        result_rows, "frame", split_axis=0, concat_axis=1, tiled=True
    ).reshape(total_rows, width)
    grad_rows = cotangent.reshape(total_rows, width)
    grad_share = lax.psum_scatter(
        lax.dot_general(
            grad_rows, temporal_attn, (((0,), (0,)), ((), ())), preferred_element_type=jnp.float32
        ).astype(jnp.bfloat16),
        "frame",
        scatter_dimension=0,
        tiled=True,
    )
    grad_out = lax.psum(grad_share, ("dp", "space")).astype(jnp.float32)
    temporal_proj = fold_rows(temporal_attn, gather_rows(temporal_out))
    block_out = (after_spatial + temporal_proj).reshape(clip_tokens.shape)
    return (block_out, grad_out)


def solution(mesh):
    placed = (
        P("dp", "frame", "space", None),
        P("dp"),
        P("dp"),
        P(),
        P("frame", None),
        P("frame", None),
        P(),
        P("frame", None),
        P("frame", None),
        P("dp", "frame", "space", None),
    )
    return jax.shard_map(
        on_device,
        mesh=mesh,
        in_specs=placed,
        out_specs=(P("dp", "frame", "space", None), P("frame", None)),
        check_vma=False,
    )
```

```python
import functools
import math

import jax
import jax.numpy as jnp
from jax import lax
from jax.experimental import pallas as pl
from jax.experimental.pallas import tpu as pltpu
from jax.sharding import PartitionSpec as P

HD = 64
PAIR = 2 * HD

norm_eps = 1e-06
score_scale = 0.125
exp2_scale = score_scale * math.log2(math.e)


def rms_norm(row_block, gain):
    values = row_block.astype(jnp.float32)
    mean_square = jnp.mean(values * values, axis=-1, keepdims=True)
    return (values * lax.rsqrt(mean_square + norm_eps) * gain).astype(jnp.bfloat16)


def fold_rows(activations, weight_rows):
    return jnp.dot(activations, weight_rows, preferred_element_type=jnp.float32)


def frame_visible(lookback, valid_frames, query_pos, key_pos):
    return (
        (key_pos <= query_pos)
        & (query_pos - key_pos < lookback)
        & ((key_pos < valid_frames) | (key_pos == query_pos))
    )


def pair_attention(query, key, value, bias=None):
    low_q = lax.broadcasted_iota(jnp.int32, query.shape, 1) < HD
    low_v = lax.broadcasted_iota(jnp.int32, value.shape, 1) < HD
    none = jnp.zeros_like(query)
    ones = jnp.ones_like(value)
    mixed = []
    for query_one, value_one in (
        (jnp.where(low_q, query, none), jnp.where(low_v, value, ones)),
        (jnp.where(low_q, none, query), jnp.where(low_v, ones, value)),
    ):
        scores = lax.dot_general(
            query_one, key, (((1,), (1,)), ((), ())), preferred_element_type=jnp.float32
        )
        if bias is not None:
            scores = scores + bias
        row_best = jnp.max(scores, axis=-1, keepdims=True)
        weights = jnp.exp2((scores - row_best) * exp2_scale).astype(jnp.bfloat16)
        mixed.append(jnp.dot(weights, value_one, preferred_element_type=jnp.float32))
    first, second = mixed
    top = jnp.where(low_q, first, second)
    bottom = pltpu.roll(jnp.where(low_q, second, first), HD, 1)
    return (top / bottom).astype(jnp.bfloat16)


def spatial_kernel(query_ref, key_ref, value_ref, out_ref, *, step):
    key, value = key_ref[...], value_ref[...]
    for start in range(0, query_ref.shape[0], step):
        out_ref[start : start + step, :] = pair_attention(
            query_ref[start : start + step, :], key, value
        )


def spatial_attention(projected, patches, width):
    rows = projected.shape[0]
    pairs = width // PAIR

    def block(shift):
        return pl.BlockSpec((patches, PAIR), lambda g, j: (g, j + shift * pairs))

    return pl.pallas_call(
        functools.partial(spatial_kernel, step=min(256, patches)),
        grid=(rows // patches, pairs),
        in_specs=[block(0), block(1), block(2)],
        out_specs=block(0),
        out_shape=jax.ShapeDtypeStruct((rows, width), jnp.bfloat16),
        compiler_params=pltpu.CompilerParams(vmem_limit_bytes=48 * 2**20),
        cost_estimate=pl.CostEstimate(
            flops=4 * rows * patches * width,
            bytes_accessed=8 * rows * width,
            transcendentals=rows * patches * width // HD,
        ),
    )(projected, projected, projected)


def temporal_kernel(bias_ref, rows_ref, out_ref, *, width):
    bias = bias_ref[...]
    frames, group, _ = out_ref.shape
    for start in range(0, width, PAIR):
        parts = [
            rows_ref[:, :, shift + start : shift + start + PAIR].reshape(frames * group, PAIR)
            for shift in (0, width, 2 * width)
        ]
        out_ref[:, :, start : start + PAIR] = pair_attention(*parts, bias).reshape(
            frames, group, PAIR
        )


def temporal_attention(projected, lookback, valid_frames, width):
    frames, patches, _ = projected.shape
    group = 16
    spots = frames * group
    row = lax.broadcasted_iota(jnp.int32, (spots, spots), 0)
    column = lax.broadcasted_iota(jnp.int32, (spots, spots), 1)
    seen = frame_visible(lookback, valid_frames, row // group, column // group)
    bias = jnp.where(seen & (row % group == column % group), 0.0, -1e30).astype(jnp.float32)
    return pl.pallas_call(
        functools.partial(temporal_kernel, width=width),
        grid=(patches // group,),
        in_specs=[
            pl.BlockSpec((spots, spots), lambda i: (0, 0)),
            pl.BlockSpec((frames, group, 3 * width), lambda i: (0, i, 0)),
        ],
        out_specs=pl.BlockSpec((frames, group, width), lambda i: (0, i, 0)),
        out_shape=jax.ShapeDtypeStruct((frames, patches, width), jnp.bfloat16),
        compiler_params=pltpu.CompilerParams(vmem_limit_bytes=48 * 2**20),
        cost_estimate=pl.CostEstimate(
            flops=4 * spots * frames * patches * width,
            bytes_accessed=8 * frames * patches * width,
            transcendentals=spots * frames * patches * width // HD,
        ),
    )(bias, projected)


def gather_rows(weight):
    return lax.all_gather(weight, "frame", axis=0, tiled=True)


def swap_frames(rows, to_patches):
    split, concat = (1, 0) if to_patches else (0, 1)
    if lax.axis_size("frame") != 2:
        return lax.all_to_all(rows, "frame", split_axis=split, concat_axis=concat, tiled=True)
    first = lax.axis_index("frame") == 0
    low, high = jnp.split(rows, 2, axis=split)
    kept = jnp.where(first, low, high)
    came = lax.ppermute(jnp.where(first, high, low), "frame", [(0, 1), (1, 0)])
    return jnp.concatenate(
        [jnp.where(first, kept, came), jnp.where(first, came, kept)], axis=concat
    )


def spatial_by_frames(tokens, gain, qkv):
    frames_here, patches_here, width = tokens.shape
    whole = lax.all_to_all(tokens, "space", split_axis=0, concat_axis=1, tiled=True)
    frames, patches, _ = whole.shape
    normed = rms_norm(whole.reshape(frames * patches, width), gain)
    projected = fold_rows(normed, qkv).astype(jnp.bfloat16)
    attended = spatial_attention(projected, patches, width).reshape(frames, patches, width)
    return lax.all_to_all(attended, "space", split_axis=1, concat_axis=0, tiled=True)


def spatial_by_heads(tokens, gain, qkv):
    frames_here, patches_here, width = tokens.shape
    parts = lax.axis_size("space")
    normed = rms_norm(tokens.reshape(-1, width), gain)
    projected = fold_rows(normed, qkv).astype(jnp.bfloat16)
    split = projected.reshape(frames_here, patches_here, 3, parts, width // parts)
    whole = lax.all_to_all(split, "space", split_axis=3, concat_axis=1, tiled=True)
    patches = whole.shape[1]
    attended = spatial_attention(
        whole.reshape(frames_here * patches, -1), patches, width // parts
    ).reshape(frames_here, patches, width // parts)
    return lax.all_to_all(attended, "space", split_axis=1, concat_axis=2, tiled=True)


def on_device(
    clip_tokens,
    lookback,
    valid_frames,
    spatial_gain,
    spatial_qkv,
    spatial_out,
    temporal_gain,
    temporal_qkv,
    temporal_out,
    cotangent,
):
    clip_count, frames_here, patches_here, width = clip_tokens.shape
    parts, frame_parts = lax.axis_size("space"), lax.axis_size("frame")
    by_frames = frames_here % parts == 0
    spatial = spatial_by_frames if by_frames else spatial_by_heads
    chunks = 2 if by_frames and frames_here % (2 * parts) == 0 else 1
    step = frames_here // chunks
    spatial_weights = gather_rows(spatial_qkv)
    spatial_out_rows = gather_rows(spatial_out)
    temporal_weights = gather_rows(temporal_qkv)
    temporal_out_rows = gather_rows(temporal_out)
    after_parts, patch_parts = [], []
    for start in range(0, frames_here, step):
        tokens = clip_tokens[0, start : start + step]
        spatial_attn = spatial(tokens, spatial_gain, spatial_weights)
        spatial_proj = fold_rows(spatial_attn.reshape(-1, width), spatial_out_rows)
        after_rows = tokens.reshape(-1, width).astype(jnp.float32) + spatial_proj
        after_parts.append(after_rows)
        patch_tokens = swap_frames(
            rms_norm(after_rows, temporal_gain).reshape(step, patches_here, width), True
        )
        patch_parts.append(patch_tokens.reshape(frame_parts, step, -1, width))
    grad_rows = swap_frames(cotangent[0], True).reshape(-1, width)
    patch_tokens = jnp.concatenate(patch_parts, axis=1)
    frames = frame_parts * frames_here
    patches = patch_tokens.shape[2]
    projected = fold_rows(
        patch_tokens.reshape(frames * patches, width), temporal_weights
    ).astype(jnp.bfloat16)
    projected, temporal_out_rows, grad_rows = lax.optimization_barrier(
        (projected, temporal_out_rows, grad_rows)
    )
    result_rows = temporal_attention(
        projected.reshape(frames, patches, 3 * width), lookback[0], valid_frames[0], width
    )
    grad_share = lax.psum_scatter(
        lax.dot_general(
            grad_rows,
            result_rows.reshape(frames * patches, width),
            (((0,), (0,)), ((), ())),
            preferred_element_type=jnp.float32,
        ).astype(jnp.bfloat16),
        "frame",
        scatter_dimension=0,
        tiled=True,
    )
    grad_out = lax.psum(grad_share, ("dp", "space")).astype(jnp.float32)
    temporal_attn = swap_frames(result_rows, False)
    block_parts = []
    for index, after_rows in enumerate(after_parts):
        rows = temporal_attn[index * step : (index + 1) * step].reshape(-1, width)
        summed = after_rows + fold_rows(rows, temporal_out_rows)
        block_parts.append(summed.reshape(1, step, patches_here, width))
    return (jnp.concatenate(block_parts, axis=1), grad_out)


def solution(mesh):
    placed = (
        P("dp", "frame", "space", None),
        P("dp"),
        P("dp"),
        P(),
        P("frame", None),
        P("frame", None),
        P(),
        P("frame", None),
        P("frame", None),
        P("dp", "frame", "space", None),
    )
    return jax.shard_map(
        on_device,
        mesh=mesh,
        in_specs=placed,
        out_specs=(P("dp", "frame", "space", None), P("frame", None)),
        check_vma=False,
    )
```
